128 devices in a mesh: freq: 32 (over y, x_lo, z), pair: 4 (over x_hi, core).
Axes of the slice: x: 4 (x_hi: 2, x_lo: 2; x = x_hi * 2 + x_lo), y: 4, z: 4, core: 2. Of those that a mesh axis runs over, the one named last changes fastest.
Arguments:
- vertex: float32 [64, 2, 48, 48, 1024], P('freq', None, None, None, 'pair'), may hold values from -6 to 6
- bubble: float32 [64, 48], P('freq'), may hold values from 0.02 to 0.2
- stencil: float32 [64, 5], P('freq'), may hold values from -3 to 3
- freq_map: int32 [48], replicated, may hold values from 0 to 47
- neighbours: int32 [8192, 3], replicated, may hold values from -1 to 1023, as said below
Outputs:
- section_vertex: float32 [64, 2, 48, 48, 1024], P('freq', None, None, None, 'pair')
The draws below stay inside these ranges and needn't reach their ends.
Inputs may be any that keep to these rules, and one draw needn't show every extreme that they name: `neighbours`: each pair index 0 to 1023 stands in column 0 of exactly 8 rows; column 1 holds any pair index; column 2 is -1 or 1.
All inputs are finite; a program needn't handle non-finite values.
Results may differ from the reference program's by a relative error of at most 0.0003.
Values sent between devices are 32-bit elements; how exact they have to be, the bound alone decides.
No kernel may reach another device: no remote copies, remote signals or barrier semaphores. Data moves between devices by JAX's collectives and lax.ppermute only.
A program may use at most 320 MiB of HBM per device.

```python
import math
import jax
import jax.numpy as jnp
from jax import lax

NW = 48
PAIRS = 1024
TERMS = 8
NS = 64
ENTRIES = 8192


def draw_neighbours(key, part):
    key = jax.random.fold_in(key, 11)
    key_partner, key_sign, key_order = jax.random.split(key, 3)
    pair_column = jnp.repeat(jnp.arange(PAIRS, dtype=jnp.int32), TERMS)
    partner_column = jax.random.randint(key_partner, (ENTRIES,), 0, PAIRS, dtype=jnp.int32)
    sign_column = 2 * jax.random.randint(key_sign, (ENTRIES,), 0, 2, dtype=jnp.int32) - 1
    table = jnp.stack([pair_column, partner_column, sign_column], axis=1)
    order = jax.random.permutation(key_order, ENTRIES)
    return table[order].astype(jnp.int32)


def plant(array, rng, low, largest):
    longest = array.shape.index(max(array.shape))
    spots = []
    for shift in (0, 1):
        where = [jax.random.randint(jax.random.fold_in(rng, axis), (), 0, length) for axis, length in enumerate(array.shape)]
        where[longest] = (where[longest] + shift) % array.shape[longest]
        spots.append(tuple(where))
    return array.at[spots[0]].set(low).at[spots[1]].set(largest)


def steps_of(own_key, shape, pieces, low, top_value):
    def one(position, blocks):
        heights = jax.random.uniform(jax.random.fold_in(jax.random.fold_in(own_key, 6), position), (blocks,), jnp.float32, low / len(pieces), top_value / len(pieces))
        return jnp.repeat(jnp.exp(heights), shape[position] // blocks).reshape((-1,) + (1,) * (len(shape) - position - 1))

    gain = one(*pieces[0])
    for cut in pieces[1:]:
        gain = gain * one(*cut)
    return gain


def normal_values(rng, shape, deviation, most, cuts=(), held_as=jnp.bfloat16):
    drawn = deviation * jax.random.normal(rng, shape, jnp.float32)
    if cuts:
        drawn = drawn * steps_of(rng, shape, cuts, -0.22, 0.18)
    return jnp.clip(drawn, -most, most).astype(held_as)


def setup_inputs(seed: int = 0) -> dict:
    arg_keys = jax.random.split(jax.random.key(seed), 6)
    return {
        "vertex": normal_values(arg_keys[0], (NS, 2, NW, NW, PAIRS), 1.0, 6.0, ((0, 32), (4, 4)), jnp.float32),
        "bubble": jnp.clip(jnp.exp(math.log(0.2) - 2.3025851 * jax.random.uniform(arg_keys[1], (NS, NW), jnp.float32) ** steps_of(arg_keys[1], (NS, NW), ((0, 32),), -0.2, 0.2)), 0.02, 0.2),
        "stencil": normal_values(arg_keys[2], (NS, 5), 0.5, 3.0, ((0, 32),), jnp.float32),
        "freq_map": plant(jax.random.randint(arg_keys[3], (NW,), 0, NW), jax.random.fold_in(arg_keys[3], 1), 0, NW - 1).astype(jnp.int32),
        "neighbours": draw_neighbours(jax.random.fold_in(arg_keys[5], 71), 0),
    }


step_size = 0.25


def reference(vertex, bubble, stencil, freq_map, neighbours):
    pair_column = neighbours[:, 0]
    partner_column = neighbours[:, 1]
    sign_column = neighbours[:, 2].astype(jnp.float32)

    def one_slot(slot):
        current = lax.dynamic_index_in_dim(vertex, slot, 0, keepdims=False)
        bubble_row = lax.dynamic_index_in_dim(bubble, slot, 0, keepdims=False)
        coeffs = lax.dynamic_index_in_dim(stencil, slot, 0, keepdims=False)
        mixed = jnp.zeros_like(current)
        for offset in range(5):
            source = slot + offset - 2
            inside = jnp.logical_and(source >= 0, source < NS).astype(jnp.float32)
            neighbour_slab = lax.dynamic_index_in_dim(vertex, jnp.clip(source, 0, NS - 1), 0, keepdims=False)
            mixed = mixed + (coeffs[offset] * inside) * neighbour_slab
        mapped = mixed[:, freq_map]
        crossed = jnp.einsum("cnwp,cwmp->cnmp", mapped * bubble_row[None, None, :, None], current, precision=lax.Precision.HIGHEST)
        spin_part = current[0]
        picked = spin_part[:, :, partner_column] * sign_column
        lattice = jnp.zeros_like(spin_part).at[:, :, pair_column].add(picked)
        lattice_term = jnp.einsum("nwp,wmp->nmp", lattice * bubble_row[None, :, None], spin_part, precision=lax.Precision.HIGHEST)
        deriv = crossed.at[0].add(-lattice_term)
        return current + step_size * deriv

    return lax.map(one_slot, jnp.arange(NS, dtype=jnp.int32))
```

```python
import functools
import jax
import jax.numpy as jnp
from jax import lax
from jax.experimental import pallas as pl
from jax.experimental.pallas import tpu as pltpu
from jax.sharding import PartitionSpec as P

step_size = 0.25
lanes = 128
sublanes = 8
row_group = 8
vmem_bytes = 48 * 1024 * 1024


def cost(microseconds):
    return pl.CostEstimate(
        flops=0, bytes_accessed=int(microseconds * 3.0e6), transcendentals=0
    )


def contract(left, right, first, write):
    depth = right.shape[0]
    tiles = right.shape[1] // sublanes
    sums = [[None] * tiles for _ in range(row_group)]
    for w in range(depth):
        columns = [right[w, sublanes * t : sublanes * (t + 1), :] for t in range(tiles)]
        for i in range(row_group):
            row = jnp.broadcast_to(left[first + i, w : w + 1, :], (sublanes, lanes))
            for t in range(tiles):
                term = row * columns[t]
                sums[i][t] = term if w == 0 else sums[i][t] + term
    for i in range(row_group):
        for t in range(tiles):
            write(i, t, sums[i][t])


def pack_kernel(rows, vertex, packed):
    def one(u, carry):
        packed[0, u] = vertex[0, 0, rows[u]]
        return carry

    lax.fori_loop(0, packed.shape[1], one, 0)


def pack(vertex, rows, component, half):
    slots, _, width, depth, _ = vertex.shape
    count = rows.shape[0]
    return pl.pallas_call(
        pack_kernel,
        grid_spec=pltpu.PrefetchScalarGridSpec(
            num_scalar_prefetch=1,
            grid=(slots,),
            in_specs=[
                pl.BlockSpec((1, 1, width, depth, lanes), lambda s, r: (s, component, 0, 0, half))
            ],
            out_specs=pl.BlockSpec((1, count, depth, lanes), lambda s, r: (s, 0, 0, 0)),
        ),
        out_shape=jax.ShapeDtypeStruct((slots, count, depth, lanes), jnp.float32),
        compiler_params=pltpu.CompilerParams(vmem_limit_bytes=vmem_bytes),
        cost_estimate=cost(3),
        name="pack",
    )(rows, vertex)


def lattice_kernel(own, partner_1, partner_2, partner_3, coupling, bubble, spin, base, out, held):
    del base
    rows, depth, pairs = held.shape
    total = jnp.zeros((rows * depth, pairs), jnp.float32)
    for j, part in enumerate((own, partner_1, partner_2, partner_3)):
        block = part[...].reshape(rows * depth, pairs)
        high = block.astype(jnp.bfloat16)
        low = (block - high.astype(jnp.float32)).astype(jnp.bfloat16)
        matrix = coupling[j]
        total = total + jnp.dot(high, matrix, preferred_element_type=jnp.float32)
        total = total + jnp.dot(low, matrix, preferred_element_type=jnp.float32)
    held[...] = total.reshape(rows, depth, pairs)
    row_0 = pl.program_id(0) * rows
    for half in range(pairs // lanes):
        columns = pl.ds(half * lanes, lanes)
        for i in range(rows):
            held[i, :, columns] = held[i, :, columns] * bubble[0]

        def write(i, t, value, columns=columns):
            tile = pl.ds(sublanes * t, sublanes)
            out[0, 0, i, tile, columns] = spin[0, 0, row_0 + i, tile, columns] - value

        contract(held.at[:, :, columns], spin.at[0, 0, :, :, columns], 0, write)


def lattice(vertex, slot, partners, coupling, bubble, base):
    slots, components, width, depth, pairs = vertex.shape
    part = pl.BlockSpec((row_group, depth, pairs), lambda j: (j, 0, 0))
    return pl.pallas_call(
        lattice_kernel,
        grid=(width // row_group,),
        in_specs=[
            pl.BlockSpec((None, None, row_group, depth, pairs), lambda j: (slot, 0, j, 0, 0)),
            part,
            part,
            part,
            pl.BlockSpec(coupling.shape, lambda j: (0, 0, 0)),
            pl.BlockSpec((1, depth, lanes), lambda j: (slot, 0, 0)),
            pl.BlockSpec((1, 1, width, depth, pairs), lambda j: (slot, 0, 0, 0, 0)),
            pl.BlockSpec(memory_space=pl.ANY),
        ],
        out_specs=pl.BlockSpec((1, 1, row_group, depth, pairs), lambda j: (slot, 0, j, 0, 0)),
        out_shape=jax.ShapeDtypeStruct(vertex.shape, jnp.float32),
        scratch_shapes=[pltpu.VMEM((row_group, depth, pairs), jnp.float32)],
        input_output_aliases={7: 0},
        compiler_params=pltpu.CompilerParams(vmem_limit_bytes=vmem_bytes),
        cost_estimate=cost(10),
        name="lattice",
    )(vertex, *partners, coupling, bubble, vertex, base)


def crossed_kernel(has_base, rows, places, stencil, vertex, before, after, bubble, *rest):
    base = rest[0]
    out, weighted, result = rest[-3:]
    slot = pl.program_id(0)
    count, depth, _ = weighted.shape
    scale = bubble[0]

    def weigh(s):
        def one(u, carry):
            row = rows[u]
            sources = (
                before[0, u],
                before[1, u],
                vertex[0, 0, row],
                vertex[1, 0, row],
                after[0, u],
                after[1, u],
            )
            mixed = stencil[s, 0] * sources[s]
            for k in range(1, 5):
                mixed = mixed + stencil[s, k] * sources[s + k]
            weighted[u] = mixed * scale
            return carry

        lax.fori_loop(0, count, one, 0)

    for s in range(2):
        pl.when(slot == s)(functools.partial(weigh, s))

    current = vertex.at[slot, 0]

    def group(j, carry):
        first = j * row_group

        def write(i, t, value):
            result[first + i, sublanes * t : sublanes * (t + 1), :] = value

        contract(weighted, current, first, write)
        return carry

    lax.fori_loop(0, count // row_group, group, 0)

    def spread(n, carry):
        start = base[0, 0, n] if has_base else current[n]
        out[0, 0, n] = start + result[places[n]]
        return carry

    lax.fori_loop(0, out.shape[2], spread, 0)


def crossed(vertex, rows, places, stencil, before, after, bubble, component, half, has_base, base):
    slots, _, width, depth, _ = vertex.shape
    count = rows.shape[0]
    whole = pl.BlockSpec((slots, count, depth, lanes), lambda s, r, q: (0, 0, 0, 0))
    block = pl.BlockSpec(
        (1, 1, width, depth, lanes), lambda s, r, q: (s, component, 0, 0, half)
    )
    held = [block if has_base else pl.BlockSpec(memory_space=pl.ANY)]
    operands = (rows, places, stencil, vertex, before, after, bubble, base)
    if base is None:
        held, operands = [], operands[:-1]
    return pl.pallas_call(
        functools.partial(crossed_kernel, has_base),
        grid_spec=pltpu.PrefetchScalarGridSpec(
            num_scalar_prefetch=2,
            grid=(slots,),
            in_specs=[
                pl.BlockSpec(memory_space=pltpu.SMEM),
                pl.BlockSpec(
                    (slots, 1, width, depth, lanes), lambda s, r, q: (0, component, 0, 0, half)
                ),
                whole,
                whole,
                pl.BlockSpec((1, depth, lanes), lambda s, r, q: (s, 0, 0)),
                *held,
            ],
            out_specs=block,
            scratch_shapes=[
                pltpu.VMEM((count, depth, lanes), jnp.float32),
                pltpu.VMEM((count, depth, lanes), jnp.float32),
            ],
        ),
        out_shape=jax.ShapeDtypeStruct(vertex.shape, jnp.float32),
        input_output_aliases={7: 0} if held else {},
        compiler_params=pltpu.CompilerParams(vmem_limit_bytes=vmem_bytes),
        cost_estimate=cost(10),
        name="crossed",
    )(*operands)


def coupling_matrices(neighbours, pair_count):
    shards = lax.axis_size("pair")
    own = lax.axis_index("pair")
    pair_column = neighbours[:, 0]
    partner_column = neighbours[:, 1]
    sign_column = neighbours[:, 2]
    inner = lax.iota(jnp.int32, pair_count)
    left_ids = jnp.concatenate([(own ^ j) * pair_count + inner for j in range(shards)])
    right_ids = own * pair_count + inner
    partner_hits = (partner_column[:, None] == left_ids[None, :]).astype(jnp.bfloat16)
    pair_hits = jnp.where(
        pair_column[:, None] == right_ids[None, :], sign_column[:, None], 0
    ).astype(jnp.bfloat16)
    signs = lax.dot_general(
        partner_hits, pair_hits, (((0,), (0,)), ((), ())), preferred_element_type=jnp.float32
    )
    return signs.astype(jnp.bfloat16).reshape(shards, pair_count, pair_count)


def body(vertex, bubble, stencil, freq_map, neighbours):
    slots, components, width, depth, pairs = vertex.shape
    rows = freq_map
    places = lax.iota(jnp.int32, width)
    shards = lax.axis_size("pair")
    devices = lax.axis_size("freq")
    onward = [(i, i + 1) for i in range(devices - 1)]
    backward = [(i + 1, i) for i in range(devices - 1)]
    across = [(i, i ^ 2) for i in range(shards)]
    beside = [(i, i ^ 1) for i in range(shards)]

    partners = []
    for slot in range(slots):
        spin = vertex[slot, 0]
        far = lax.ppermute(spin, "pair", across)
        near = lax.ppermute(spin, "pair", beside)
        partners.append((near, far, lax.ppermute(far, "pair", beside)))
    chunks = [(1, 0), (1, 1), (0, 0), (0, 1)]
    sides = {}
    for component, half in chunks:
        packed = pack(vertex, rows, component, half)
        sides[component, half] = (
            lax.ppermute(packed, "freq", onward),
            lax.ppermute(packed, "freq", backward),
        )
    scaled = jnp.broadcast_to(
        (step_size * bubble)[:, :, None], (slots, depth, lanes)
    )
    coupling = coupling_matrices(neighbours, pairs)
    section = None
    for component, half in chunks:
        if (component, half) == (0, 0):
            for slot in range(slots):
                section = lattice(vertex, slot, partners[slot], coupling, scaled, section)
        section = crossed(
            vertex, rows, places, stencil, *sides[component, half], scaled, component, half,
            component == 0, section,
        )
    return section


def solution(mesh):
    in_specs = (P("freq", None, None, None, "pair"), P("freq", None), P("freq", None), P(), P())
    out_specs = P("freq", None, None, None, "pair")
    return jax.shard_map(body, mesh=mesh, in_specs=in_specs, out_specs=out_specs, check_vma=False)
```

```python
import functools
import jax
import jax.numpy as jnp
from jax import lax
from jax.experimental import pallas as pl
from jax.experimental.pallas import tpu as pltpu
from jax.sharding import PartitionSpec as P

step_size = 0.25
lanes = 128
sublanes = 8
row_group = 8
row_step = 8
depth_z = 4
vmem_bytes = 48 * 1024 * 1024


def cost(microseconds):
    return pl.CostEstimate(
        flops=0, bytes_accessed=int(microseconds * 3.0e3), transcendentals=0
    )


def contract(left, right, first, write):
    depth = right.shape[0]
    tiles = right.shape[1] // sublanes
    sums = [[None] * tiles for _ in range(row_group)]
    for w in range(depth):
        columns = [right[w, sublanes * t : sublanes * (t + 1), :] for t in range(tiles)]
        for i in range(row_group):
            row = jnp.broadcast_to(left[first + i, w : w + 1, :], (sublanes, lanes))
            for t in range(tiles):
                term = row * columns[t]
                sums[i][t] = term if w == 0 else sums[i][t] + term
    for i in range(row_group):
        for t in range(tiles):
            write(i, t, sums[i][t])


def pack_kernel(rows, vertex, packed):
    def one(u, carry):
        packed[0, u] = vertex[0, 0, rows[u]]
        return carry

    lax.fori_loop(0, packed.shape[1], one, 0)


def pack(vertex, rows, component, half=None):
    slots, _, width, depth, pairs = vertex.shape
    columns = pairs if half is None else lanes
    place = half or 0
    count = rows.shape[0]
    return pl.pallas_call(
        pack_kernel,
        grid_spec=pltpu.PrefetchScalarGridSpec(
            num_scalar_prefetch=1,
            grid=(slots,),
            in_specs=[
                pl.BlockSpec(
                    (1, 1, width, depth, columns), lambda s, r: (s, component, 0, 0, place)
                )
            ],
            out_specs=pl.BlockSpec((1, count, depth, columns), lambda s, r: (s, 0, 0, 0)),
        ),
        out_shape=jax.ShapeDtypeStruct((slots, count, depth, columns), jnp.float32),
        compiler_params=pltpu.CompilerParams(vmem_limit_bytes=vmem_bytes),
        cost_estimate=cost(3),
        name="pack",
    )(rows, vertex)


def lattice_kernel(own, near, far, far_near, coupling, bubble, spin, out, held):
    rows, depth, pairs = held.shape
    total = jnp.zeros((rows * depth, pairs), jnp.float32)
    for j, part in enumerate((own, near, far, far_near)):
        block = part[...].reshape(rows * depth, pairs)
        high = block.astype(jnp.bfloat16)
        low = (block - high.astype(jnp.float32)).astype(jnp.bfloat16)
        matrix = coupling[j]
        total = total + jnp.dot(high, matrix, preferred_element_type=jnp.float32)
        total = total + jnp.dot(low, matrix, preferred_element_type=jnp.float32)
    held[...] = total.reshape(rows, depth, pairs)
    row_0 = pl.program_id(1) * rows
    for half in range(pairs // lanes):
        columns = pl.ds(half * lanes, lanes)
        for i in range(rows):
            held[i, :, columns] = held[i, :, columns] * bubble[0]

        def write(i, t, value, columns=columns):
            tile = pl.ds(sublanes * t, sublanes)
            out[0, 0, i, tile, columns] = spin[0, 0, row_0 + i, tile, columns] - value

        contract(held.at[:, :, columns], spin.at[0, 0, :, :, columns], 0, write)


def lattice(vertex, near, far, far_near, coupling, bubble):
    slots, components, width, depth, pairs = vertex.shape
    part = pl.BlockSpec((None, row_group, depth, pairs), lambda s, j: (s, j, 0, 0))
    return pl.pallas_call(
        lattice_kernel,
        grid=(slots, width // row_group),
        in_specs=[
            pl.BlockSpec((None, None, row_group, depth, pairs), lambda s, j: (s, 0, j, 0, 0)),
            part,
            part,
            part,
            pl.BlockSpec(coupling.shape, lambda s, j: (0, 0, 0)),
            pl.BlockSpec((1, depth, lanes), lambda s, j: (s, 0, 0)),
            pl.BlockSpec((1, 1, width, depth, pairs), lambda s, j: (s, 0, 0, 0, 0)),
        ],
        out_specs=pl.BlockSpec((1, 1, row_group, depth, pairs), lambda s, j: (s, 0, j, 0, 0)),
        out_shape=jax.ShapeDtypeStruct(vertex.shape, jnp.float32),
        scratch_shapes=[pltpu.VMEM((row_group, depth, pairs), jnp.float32)],
        compiler_params=pltpu.CompilerParams(vmem_limit_bytes=vmem_bytes),
        cost_estimate=cost(28),
        name="lattice",
    )(vertex, near, far, far_near, coupling, bubble, vertex)


def crossed_kernel(
    has_relay, has_base, rows, places, stencil, vertex, before, after, bubble, *rest
):
    relay = rest[0]
    base = rest[1 if has_relay else 0]
    out, weighted, result = rest[-3:]
    slot = pl.program_id(0)
    count = before.shape[1]
    groups = weighted.shape[0] // row_group
    scale = bubble[0]

    if has_relay:
        plane = lax.axis_index("freq") % depth_z

    def side(direct, s, u, end):
        if has_relay:
            return jnp.where(plane == end, relay[s, u], direct[s, u])
        return direct[s, u]

    def weigh(s):
        def one(u, carry):
            row = rows[u]
            sources = (
                side(before, 0, u, 0),
                side(before, 1, u, 0),
                vertex[0, 0, row],
                vertex[1, 0, row],
                side(after, 0, u, depth_z - 1),
                side(after, 1, u, depth_z - 1),
            )
            mixed = stencil[s, 0] * sources[s]
            for k in range(1, 5):
                mixed = mixed + stencil[s, k] * sources[s + k]
            weighted[u] = mixed * scale
            return carry

        lax.fori_loop(0, count, one, 0)

    for s in range(2):
        pl.when(slot == s)(functools.partial(weigh, s))

    current = vertex.at[slot, 0]

    def group(j, carry):
        first = j * row_group

        def write(i, t, value):
            result[first + i, sublanes * t : sublanes * (t + 1), :] = value

        contract(weighted, current, first, write)
        return carry

    lax.fori_loop(0, groups, group, 0)

    def spread(n, carry):
        start = base[0, 0, n] if has_base else current[n]
        out[0, 0, n] = start + result[places[n]]
        return carry

    lax.fori_loop(0, out.shape[2], spread, 0)


def crossed(
    vertex, rows, places, stencil, before, after, bubble, component, half, has_base, base, relay=None
):
    slots, _, width, depth, _ = vertex.shape
    count = rows.shape[0]
    padded = -(-count // row_group) * row_group
    shape = (slots, count, depth, lanes)
    whole = pl.BlockSpec(shape, lambda s, r, q: (0, 0, 0, 0))
    place = half if before.shape[3] > lanes else 0
    beside = pl.BlockSpec(shape, lambda s, r, q: (0, 0, 0, place))
    block = pl.BlockSpec(
        (1, 1, width, depth, lanes), lambda s, r, q: (s, component, 0, 0, half)
    )
    specs = [
        pl.BlockSpec(memory_space=pltpu.SMEM),
        pl.BlockSpec((slots, 1, width, depth, lanes), lambda s, r, q: (0, component, 0, 0, half)),
        beside,
        beside,
        pl.BlockSpec((1, depth, lanes), lambda s, r, q: (s, 0, 0)),
    ]
    operands = [rows, places, stencil, vertex, before, after, bubble]
    if relay is not None:
        specs.append(whole)
        operands.append(relay)
    if base is not None:
        specs.append(block if has_base else pl.BlockSpec(memory_space=pl.ANY))
        operands.append(base)
    return pl.pallas_call(
        functools.partial(crossed_kernel, relay is not None, has_base),
        grid_spec=pltpu.PrefetchScalarGridSpec(
            num_scalar_prefetch=2,
            grid=(slots,),
            in_specs=specs,
            out_specs=block,
            scratch_shapes=[
                pltpu.VMEM((padded, depth, lanes), jnp.float32),
                pltpu.VMEM((padded, depth, lanes), jnp.float32),
            ],
        ),
        out_shape=jax.ShapeDtypeStruct(vertex.shape, jnp.float32),
        input_output_aliases={} if base is None else {len(operands) - 1: 0},
        compiler_params=pltpu.CompilerParams(vmem_limit_bytes=vmem_bytes),
        cost_estimate=cost(10),
        name="crossed",
    )(*operands)


def coupling_matrices(neighbours, pair_count):
    shards = lax.axis_size("pair")
    own = lax.axis_index("pair")
    pair_column = neighbours[:, 0]
    partner_column = neighbours[:, 1]
    sign_column = neighbours[:, 2]
    inner = lax.iota(jnp.int32, pair_count)
    left_ids = jnp.concatenate([(own ^ j) * pair_count + inner for j in range(shards)])
    right_ids = own * pair_count + inner
    partner_hits = (partner_column[:, None] == left_ids[None, :]).astype(jnp.bfloat16)
    pair_hits = jnp.where(
        pair_column[:, None] == right_ids[None, :], sign_column[:, None], 0
    ).astype(jnp.bfloat16)
    signs = lax.dot_general(
        partner_hits, pair_hits, (((0,), (0,)), ((), ())), preferred_element_type=jnp.float32
    )
    return signs.astype(jnp.bfloat16).reshape(shards, pair_count, pair_count)


def section_of(vertex, bubble, stencil, rows, places, neighbours):
    slots, components, width, depth, pairs = vertex.shape
    shards = lax.axis_size("pair")
    devices = lax.axis_size("freq")
    last = depth_z - 1
    onward = [(i, i + 1) for i in range(devices - 1)]
    backward = [(j, i) for i, j in onward]
    onward_inside = [(i, j) for i, j in onward if i % depth_z != last]
    backward_inside = [(j, i) for i, j in onward_inside]
    steps = [(i, j) for i, j in onward if i % depth_z == last]
    lend = [(i, i - 1) for i, _ in steps] + [(j, j + 1) for _, j in steps]
    wrap = [(i, i - last) for i, _ in steps] + [(j, j + last) for _, j in steps]
    sideways = [(i - last, j) for i, j in steps] + [(j + last, i) for i, j in steps]
    relay = [(i - 1, j) for i, j in steps] + [(j + 1, i) for i, j in steps]
    across = [(i, i ^ 2) for i in range(shards)]
    beside = [(i, i ^ 1) for i in range(shards)]
    chunks = [(1, 0), (1, 1), (0, 0), (0, 1)]

    def add(section, j, sides, turned=None):
        component, half = chunks[j]
        return crossed(
            vertex, rows, places, stencil, *sides, scaled, component, half,
            component == 0, section, turned,
        )

    def halo(packed):
        return lax.ppermute(packed, "freq", onward), lax.ppermute(packed, "freq", backward)

    spin = vertex[:, 0]
    scaled = jnp.broadcast_to((step_size * bubble)[:, :, None], (slots, depth, lanes))
    packed = [pack(vertex, rows, component, half) for component, half in chunks]
    density = pack(vertex, rows, 1)
    near = lax.ppermute(spin, "pair", beside)
    stage = (
        lax.ppermute(spin, "pair", across),
        near,
        lax.ppermute(packed[0], "freq", lend),
        lax.ppermute(density, "freq", onward_inside),
        lax.ppermute(density, "freq", backward_inside),
        lax.ppermute(lax.optimization_barrier((packed[1], near))[0], "freq", wrap),
        coupling_matrices(neighbours, pairs),
        *packed[2:],
    )
    far, near, lent, before, behind, wrapped, coupling, *packed = lax.optimization_barrier(stage)
    stage = (
        lax.ppermute(lent, "freq", relay),
        lax.ppermute(wrapped, "freq", sideways),
        *halo(packed[0]),
        lattice(vertex, near, far, lax.ppermute(far, "pair", beside), coupling, scaled),
        packed[1],
    )
    relayed, turned, *sides_2, section, packed_3 = lax.optimization_barrier(stage)
    sides_3 = halo(packed_3)
    section = add(section, 0, (before, behind), relayed)
    section = add(section, 1, (before, behind), turned)
    section = add(section, 2, sides_2)
    return add(section, 3, sides_3)


def body(vertex, bubble, stencil, freq_map, neighbours):
    width = vertex.shape[2]
    ids = lax.iota(jnp.int32, width)
    picked = freq_map[:, None] == ids[None, :]
    used = jnp.any(picked, axis=0)
    rank = jnp.sum(jnp.where(used[:, None] & (ids[:, None] <= ids[None, :]), 1, 0), axis=0) - 1
    rows = jnp.sum(jnp.where(used[:, None] & (rank[:, None] == ids[None, :]), ids[:, None], 0), axis=0)
    places = jnp.sum(jnp.where(picked, rank[None, :], 0), axis=1)
    count = rank[width - 1] + 1

    def case(size):
        return lambda: section_of(vertex, bubble, stencil, rows[:size], places, neighbours)

    return lax.switch(
        (count - 1) // row_step, [case(size) for size in range(row_step, width + 1, row_step)]
    )


def solution(mesh):
    in_specs = (P("freq", None, None, None, "pair"), P("freq", None), P("freq", None), P(), P())
    out_specs = P("freq", None, None, None, "pair")
    return jax.shard_map(body, mesh=mesh, in_specs=in_specs, out_specs=out_specs, check_vma=False)
```

```python
import functools
import jax
import jax.numpy as jnp
from jax import lax
from jax.experimental import pallas as pl
from jax.experimental.pallas import tpu as pltpu
from jax.sharding import PartitionSpec as P

step_size = 0.25
lanes = 128
sublanes = 8
row_group = 8
main_rows = 34
depth_z = 4
vmem_bytes = 48 * 1024 * 1024


def cost(microseconds):
    return pl.CostEstimate(
        flops=0, bytes_accessed=int(microseconds * 3.0e3), transcendentals=0
    )


def group_of(count):
    return min((8, 6), key=lambda size: -(-count // size) * size)


def contract(left, right, first, rows, write):
    depth = right.shape[0]
    tiles = right.shape[1] // sublanes
    sums = [[None] * tiles for _ in range(rows)]
    for w in range(depth):
        columns = [right[w, sublanes * t : sublanes * (t + 1), :] for t in range(tiles)]
        for i in range(rows):
            row = jnp.broadcast_to(left[first + i, w : w + 1, :], (sublanes, lanes))
            for t in range(tiles):
                term = row * columns[t]
                sums[i][t] = term if w == 0 else sums[i][t] + term
    for i in range(rows):
        for t in range(tiles):
            write(i, t, sums[i][t])


def pack_kernel(rows, vertex, packed):
    def one(u, carry):
        packed[0, u] = vertex[0, 0, rows[u]]
        return carry

    lax.fori_loop(0, packed.shape[1], one, 0)


def pack(vertex, rows, component, half=None):
    slots, _, width, depth, pairs = vertex.shape
    columns = pairs if half is None else lanes
    place = half or 0
    count = rows.shape[0]
    return pl.pallas_call(
        pack_kernel,
        grid_spec=pltpu.PrefetchScalarGridSpec(
            num_scalar_prefetch=1,
            grid=(slots,),
            in_specs=[
                pl.BlockSpec(
                    (1, 1, width, depth, columns), lambda s, r: (s, component, 0, 0, place)
                )
            ],
            out_specs=pl.BlockSpec((1, count, depth, columns), lambda s, r: (s, 0, 0, 0)),
        ),
        out_shape=jax.ShapeDtypeStruct((slots, count, depth, columns), jnp.float32),
        compiler_params=pltpu.CompilerParams(vmem_limit_bytes=vmem_bytes),
        cost_estimate=cost(3),
        name="pack",
    )(rows, vertex)


def lattice_kernel(own, near, far, far_near, coupling, bubble, spin, out, held):
    rows, depth, pairs = held.shape
    total = jnp.zeros((rows * depth, pairs), jnp.float32)
    for j, part in enumerate((own, near, far, far_near)):
        block = part[...].reshape(rows * depth, pairs)
        high = block.astype(jnp.bfloat16)
        low = (block - high.astype(jnp.float32)).astype(jnp.bfloat16)
        matrix = coupling[j]
        total = total + jnp.dot(high, matrix, preferred_element_type=jnp.float32)
        total = total + jnp.dot(low, matrix, preferred_element_type=jnp.float32)
    held[...] = total.reshape(rows, depth, pairs)
    row_0 = pl.program_id(1) * rows
    for half in range(pairs // lanes):
        columns = pl.ds(half * lanes, lanes)
        for i in range(rows):
            held[i, :, columns] = held[i, :, columns] * bubble[0]

        def write(i, t, value, columns=columns):
            tile = pl.ds(sublanes * t, sublanes)
            out[0, 0, i, tile, columns] = spin[0, 0, row_0 + i, tile, columns] - value

        contract(held.at[:, :, columns], spin.at[0, 0, :, :, columns], 0, rows, write)


def lattice(vertex, near, far, far_near, coupling, bubble):
    slots, components, width, depth, pairs = vertex.shape
    part = pl.BlockSpec((None, row_group, depth, pairs), lambda s, j: (s, j, 0, 0))
    return pl.pallas_call(
        lattice_kernel,
        grid=(slots, width // row_group),
        in_specs=[
            pl.BlockSpec((None, None, row_group, depth, pairs), lambda s, j: (s, 0, j, 0, 0)),
            part,
            part,
            part,
            pl.BlockSpec(coupling.shape, lambda s, j: (0, 0, 0)),
            pl.BlockSpec((1, depth, lanes), lambda s, j: (s, 0, 0)),
            pl.BlockSpec((1, 1, width, depth, pairs), lambda s, j: (s, 0, 0, 0, 0)),
        ],
        out_specs=pl.BlockSpec((1, 1, row_group, depth, pairs), lambda s, j: (s, 0, j, 0, 0)),
        out_shape=jax.ShapeDtypeStruct(vertex.shape, jnp.float32),
        scratch_shapes=[pltpu.VMEM((row_group, depth, pairs), jnp.float32)],
        compiler_params=pltpu.CompilerParams(vmem_limit_bytes=vmem_bytes),
        cost_estimate=cost(28),
        name="lattice",
    )(vertex, near, far, far_near, coupling, bubble, vertex)


def crossed_kernel(
    has_relay, has_base, rows, places, stencil, vertex, before, after, bubble, *rest
):
    relay = rest[0]
    base = rest[1 if has_relay else 0]
    out, weighted, result = rest[-3:]
    slot = pl.program_id(0)
    count = before.shape[1]
    size = group_of(count)
    scale = bubble[0]

    if has_relay:
        plane = lax.axis_index("freq") % depth_z

    def side(direct, s, u, end):
        if has_relay:
            return jnp.where(plane == end, relay[s, u], direct[s, u])
        return direct[s, u]

    def weigh(s):
        def one(u, carry):
            row = rows[u]
            sources = (
                side(before, 0, u, 0),
                side(before, 1, u, 0),
                vertex[0, 0, row],
                vertex[1, 0, row],
                side(after, 0, u, depth_z - 1),
                side(after, 1, u, depth_z - 1),
            )
            mixed = stencil[s, 0] * sources[s]
            for k in range(1, 5):
                mixed = mixed + stencil[s, k] * sources[s + k]
            weighted[u] = mixed * scale
            return carry

        lax.fori_loop(0, count, one, 0)

    for s in range(2):
        pl.when(slot == s)(functools.partial(weigh, s))

    current = vertex.at[slot, 0]

    def group(j, carry):
        first = j * size

        def write(i, t, value):
            result[first + i, sublanes * t : sublanes * (t + 1), :] = value

        contract(weighted, current, first, size, write)
        return carry

    lax.fori_loop(0, weighted.shape[0] // size, group, 0)

    def spread(n, carry):
        start = base[0, 0, n] if has_base else current[n]
        place = places[n]
        inside = (place >= 0) & (place < count)
        row = result[jnp.where(inside, place, 0)]
        out[0, 0, n] = start + jnp.where(inside, row, jnp.zeros_like(row))
        return carry

    lax.fori_loop(0, out.shape[2], spread, 0)


def crossed(
    vertex, rows, places, stencil, before, after, bubble, component, half, has_base, base, relay=None
):
    slots, _, width, depth, _ = vertex.shape
    count = rows.shape[0]
    size = group_of(count)
    padded = -(-count // size) * size
    shape = (slots, count, depth, lanes)
    whole = pl.BlockSpec(shape, lambda s, r, q: (0, 0, 0, 0))
    place = half if before.shape[3] > lanes else 0
    beside = pl.BlockSpec(shape, lambda s, r, q: (0, 0, 0, place))
    block = pl.BlockSpec(
        (1, 1, width, depth, lanes), lambda s, r, q: (s, component, 0, 0, half)
    )
    specs = [
        pl.BlockSpec(memory_space=pltpu.SMEM),
        pl.BlockSpec((slots, 1, width, depth, lanes), lambda s, r, q: (0, component, 0, 0, half)),
        beside,
        beside,
        pl.BlockSpec((1, depth, lanes), lambda s, r, q: (s, 0, 0)),
    ]
    operands = [rows, places, stencil, vertex, before, after, bubble]
    if relay is not None:
        specs.append(whole)
        operands.append(relay)
    if base is not None:
        specs.append(block if has_base else pl.BlockSpec(memory_space=pl.ANY))
        operands.append(base)
    return pl.pallas_call(
        functools.partial(crossed_kernel, relay is not None, has_base),
        grid_spec=pltpu.PrefetchScalarGridSpec(
            num_scalar_prefetch=2,
            grid=(slots,),
            in_specs=specs,
            out_specs=block,
            scratch_shapes=[
                pltpu.VMEM((padded, depth, lanes), jnp.float32),
                pltpu.VMEM((padded, depth, lanes), jnp.float32),
            ],
        ),
        out_shape=jax.ShapeDtypeStruct(vertex.shape, jnp.float32),
        input_output_aliases={} if base is None else {len(operands) - 1: 0},
        compiler_params=pltpu.CompilerParams(vmem_limit_bytes=vmem_bytes),
        cost_estimate=cost(10),
        name="crossed",
    )(*operands)


def coupling_matrices(neighbours, pair_count):
    shards = lax.axis_size("pair")
    own = lax.axis_index("pair")
    pair_column = neighbours[:, 0]
    partner_column = neighbours[:, 1]
    sign_column = neighbours[:, 2]
    inner = lax.iota(jnp.int32, pair_count)
    left_ids = jnp.concatenate([(own ^ j) * pair_count + inner for j in range(shards)])
    right_ids = own * pair_count + inner
    partner_hits = (partner_column[:, None] == left_ids[None, :]).astype(jnp.bfloat16)
    pair_hits = jnp.where(
        pair_column[:, None] == right_ids[None, :], sign_column[:, None], 0
    ).astype(jnp.bfloat16)
    signs = lax.dot_general(
        partner_hits, pair_hits, (((0,), (0,)), ((), ())), preferred_element_type=jnp.float32
    )
    return signs.astype(jnp.bfloat16).reshape(shards, pair_count, pair_count)


def section_of(vertex, bubble, stencil, rows, places, more, neighbours):
    slots, components, width, depth, pairs = vertex.shape
    shards = lax.axis_size("pair")
    devices = lax.axis_size("freq")
    last = depth_z - 1
    onward = [(i, i + 1) for i in range(devices - 1)]
    backward = [(j, i) for i, j in onward]
    onward_inside = [(i, j) for i, j in onward if i % depth_z != last]
    backward_inside = [(j, i) for i, j in onward_inside]
    steps = [(i, j) for i, j in onward if i % depth_z == last]
    lend = [(i, i - 1) for i, _ in steps] + [(j, j + 1) for _, j in steps]
    wrap = [(i, i - last) for i, _ in steps] + [(j, j + last) for _, j in steps]
    sideways = [(i - last, j) for i, j in steps] + [(j + last, i) for i, j in steps]
    relay = [(i - 1, j) for i, j in steps] + [(j + 1, i) for i, j in steps]
    across = [(i, i ^ 2) for i in range(shards)]
    beside = [(i, i ^ 1) for i in range(shards)]
    chunks = [(1, 0), (1, 1), (0, 0), (0, 1)]

    every_row, rows = rows, rows[:main_rows]

    def add(section, j, sides, turned=None):
        component, half = chunks[j]
        return crossed(
            vertex, rows, places, stencil, *sides, scaled, component, half,
            component == 0, section, turned,
        )

    def add_more(turn, section):
        first = (turn + 1) * main_rows
        more_rows = lax.dynamic_slice(every_row, (first,), (width - main_rows,))
        for component, half in chunks:
            section = crossed(
                vertex, more_rows, places - first, stencil,
                *halo(pack(vertex, more_rows, component, half)), scaled, component, half,
                True, section,
            )
        return section

    def halo(packed):
        return lax.ppermute(packed, "freq", onward), lax.ppermute(packed, "freq", backward)

    spin = vertex[:, 0]
    scaled = jnp.broadcast_to((step_size * bubble)[:, :, None], (slots, depth, lanes))
    packed = [pack(vertex, rows, component, half) for component, half in chunks]
    density = pack(vertex, rows, 1)
    near = lax.ppermute(spin, "pair", beside)
    stage = (
        lax.ppermute(spin, "pair", across),
        near,
        lax.ppermute(packed[0], "freq", lend),
        lax.ppermute(density, "freq", onward_inside),
        lax.ppermute(density, "freq", backward_inside),
        lax.ppermute(lax.optimization_barrier((packed[1], near))[0], "freq", wrap),
        coupling_matrices(neighbours, pairs),
        *packed[2:],
    )
    far, near, lent, before, behind, wrapped, coupling, *packed = lax.optimization_barrier(stage)
    section = lattice(vertex, near, far, lax.ppermute(far, "pair", beside), coupling, scaled)
    section = add(section, 1, (before, behind), lax.ppermute(wrapped, "freq", sideways))
    stage = (lax.ppermute(lent, "freq", relay), *halo(packed[0]), section, packed[1])
    relayed, *sides_2, section, packed_3 = lax.optimization_barrier(stage)
    sides_3 = halo(packed_3)
    section = add(section, 0, (before, behind), relayed)
    section = add(section, 2, sides_2)
    section = add(section, 3, sides_3)
    return lax.fori_loop(0, more, add_more, section)


def body(vertex, bubble, stencil, freq_map, neighbours):
    width = vertex.shape[2]
    ids = lax.iota(jnp.int32, width)
    picked = freq_map[:, None] == ids[None, :]
    used = jnp.any(picked, axis=0)
    rank = jnp.sum(jnp.where(used[:, None] & (ids[:, None] <= ids[None, :]), 1, 0), axis=0) - 1
    rows = jnp.sum(jnp.where(used[:, None] & (rank[:, None] == ids[None, :]), ids[:, None], 0), axis=0)
    places = jnp.sum(jnp.where(picked, rank[None, :], 0), axis=1)
    count = rank[width - 1] + 1

    more = (count > main_rows).astype(jnp.int32)
    return section_of(vertex, bubble, stencil, rows, places, more, neighbours)


def solution(mesh):
    in_specs = (P("freq", None, None, None, "pair"), P("freq", None), P("freq", None), P(), P())
    out_specs = P("freq", None, None, None, "pair")
    return jax.shard_map(body, mesh=mesh, in_specs=in_specs, out_specs=out_specs, check_vma=False)
```

```python
import functools
import jax
import jax.numpy as jnp
from jax import lax
from jax.experimental import pallas as pl
from jax.experimental.pallas import tpu as pltpu
from jax.sharding import PartitionSpec as P

step_size = 0.25
lanes = 128
sublanes = 8
row_group = 8
main_rows = 34
depth_z = 4
vmem_bytes = 48 * 1024 * 1024


def cost(microseconds):
    return pl.CostEstimate(
        flops=0, bytes_accessed=int(microseconds * 3.0e3), transcendentals=0
    )


def group_of(count):
    return min((8, 6), key=lambda size: -(-count // size) * size)


def contract(left, right, first, rows, write):
    depth = right.shape[0]
    tiles = right.shape[1] // sublanes
    sums = [[None] * tiles for _ in range(rows)]
    for w in range(depth):
        columns = [right[w, sublanes * t : sublanes * (t + 1), :] for t in range(tiles)]
        for i in range(rows):
            row = jnp.broadcast_to(left[first + i, w : w + 1, :], (sublanes, lanes))
            for t in range(tiles):
                term = row * columns[t]
                sums[i][t] = term if w == 0 else sums[i][t] + term
    for i in range(rows):
        for t in range(tiles):
            write(i, t, sums[i][t])


def pack_kernel(rows, vertex, packed):
    def one(u, carry):
        packed[0, u] = vertex[0, 0, rows[u]]
        return carry

    lax.fori_loop(0, packed.shape[1], one, 0)


def pack(vertex, rows, component, half=None):
    slots, _, width, depth, pairs = vertex.shape
    columns = pairs if half is None else lanes
    place = half or 0
    count = rows.shape[0]
    return pl.pallas_call(
        pack_kernel,
        grid_spec=pltpu.PrefetchScalarGridSpec(
            num_scalar_prefetch=1,
            grid=(slots,),
            in_specs=[
                pl.BlockSpec(
                    (1, 1, width, depth, columns), lambda s, r: (s, component, 0, 0, place)
                )
            ],
            out_specs=pl.BlockSpec((1, count, depth, columns), lambda s, r: (s, 0, 0, 0)),
        ),
        out_shape=jax.ShapeDtypeStruct((slots, count, depth, columns), jnp.float32),
        compiler_params=pltpu.CompilerParams(vmem_limit_bytes=vmem_bytes),
        cost_estimate=cost(3),
        name="pack",
    )(rows, vertex)


def lattice_kernel(own, near, far, far_near, coupling, bubble, spin, out, held):
    rows, depth, pairs = held.shape
    total = jnp.zeros((rows * depth, pairs), jnp.float32)
    for j, part in enumerate((own, near, far, far_near)):
        block = part[...].reshape(rows * depth, pairs)
        high = block.astype(jnp.bfloat16)
        low = (block - high.astype(jnp.float32)).astype(jnp.bfloat16)
        matrix = coupling[j]
        total = total + jnp.dot(high, matrix, preferred_element_type=jnp.float32)
        total = total + jnp.dot(low, matrix, preferred_element_type=jnp.float32)
    held[...] = total.reshape(rows, depth, pairs)
    row_0 = pl.program_id(1) * rows
    for half in range(pairs // lanes):
        columns = pl.ds(half * lanes, lanes)
        for i in range(rows):
            held[i, :, columns] = held[i, :, columns] * bubble[0]

        def write(i, t, value, columns=columns):
            tile = pl.ds(sublanes * t, sublanes)
            out[0, 0, i, tile, columns] = spin[0, 0, row_0 + i, tile, columns] - value

        contract(held.at[:, :, columns], spin.at[0, 0, :, :, columns], 0, rows, write)


def lattice(vertex, near, far, far_near, coupling, bubble):
    slots, components, width, depth, pairs = vertex.shape
    part = pl.BlockSpec((None, row_group, depth, pairs), lambda s, j: (s, j, 0, 0))
    return pl.pallas_call(
        lattice_kernel,
        grid=(slots, width // row_group),
        in_specs=[
            pl.BlockSpec((None, None, row_group, depth, pairs), lambda s, j: (s, 0, j, 0, 0)),
            part,
            part,
            part,
            pl.BlockSpec(coupling.shape, lambda s, j: (0, 0, 0)),
            pl.BlockSpec((1, depth, lanes), lambda s, j: (s, 0, 0)),
            pl.BlockSpec((1, 1, width, depth, pairs), lambda s, j: (s, 0, 0, 0, 0)),
        ],
        out_specs=pl.BlockSpec((1, 1, row_group, depth, pairs), lambda s, j: (s, 0, j, 0, 0)),
        out_shape=jax.ShapeDtypeStruct(vertex.shape, jnp.float32),
        scratch_shapes=[pltpu.VMEM((row_group, depth, pairs), jnp.float32)],
        compiler_params=pltpu.CompilerParams(vmem_limit_bytes=vmem_bytes),
        cost_estimate=cost(28),
        name="lattice",
    )(vertex, near, far, far_near, coupling, bubble, vertex)


def crossed_kernel(
    has_relay, has_base, rows, places, stencil, vertex, before, after, bubble, *rest
):
    relay = rest[0]
    base = rest[1 if has_relay else 0]
    out, weighted, result = rest[-3:]
    slot = pl.program_id(0)
    count = before.shape[1]
    size = group_of(count)
    scale = bubble[0]

    if has_relay:
        plane = lax.axis_index("freq") % depth_z

    def side(direct, s, u, end):
        if has_relay:
            return jnp.where(plane == end, relay[s, u], direct[s, u])
        return direct[s, u]

    def weigh(s):
        def one(u, carry):
            row = rows[u]
            sources = (
                side(before, 0, u, 0),
                side(before, 1, u, 0),
                vertex[0, 0, row],
                vertex[1, 0, row],
                side(after, 0, u, depth_z - 1),
                side(after, 1, u, depth_z - 1),
            )
            mixed = stencil[s, 0] * sources[s]
            for k in range(1, 5):
                mixed = mixed + stencil[s, k] * sources[s + k]
            weighted[u] = mixed * scale
            return carry

        lax.fori_loop(0, count, one, 0)

    for s in range(2):
        pl.when(slot == s)(functools.partial(weigh, s))

    current = vertex.at[slot, 0]

    def group(j, carry):
        first = j * size

        def write(i, t, value):
            result[first + i, sublanes * t : sublanes * (t + 1), :] = value

        contract(weighted, current, first, size, write)
        return carry

    lax.fori_loop(0, weighted.shape[0] // size, group, 0)

    def spread(n, carry):
        start = base[0, 0, n] if has_base else current[n]
        place = places[n]
        inside = (place >= 0) & (place < count)
        row = result[jnp.where(inside, place, 0)]
        out[0, 0, n] = start + jnp.where(inside, row, jnp.zeros_like(row))
        return carry

    lax.fori_loop(0, out.shape[2], spread, 0)


def crossed(
    vertex, rows, places, stencil, before, after, bubble, component, half, has_base, base, relay=None
):
    slots, _, width, depth, _ = vertex.shape
    count = rows.shape[0]
    size = group_of(count)
    padded = -(-count // size) * size
    shape = (slots, count, depth, lanes)
    whole = pl.BlockSpec(shape, lambda s, r, q: (0, 0, 0, 0))
    place = half if before.shape[3] > lanes else 0
    beside = pl.BlockSpec(shape, lambda s, r, q: (0, 0, 0, place))
    block = pl.BlockSpec(
        (1, 1, width, depth, lanes), lambda s, r, q: (s, component, 0, 0, half)
    )
    specs = [
        pl.BlockSpec(memory_space=pltpu.SMEM),
        pl.BlockSpec((slots, 1, width, depth, lanes), lambda s, r, q: (0, component, 0, 0, half)),
        beside,
        beside,
        pl.BlockSpec((1, depth, lanes), lambda s, r, q: (s, 0, 0)),
    ]
    operands = [rows, places, stencil, vertex, before, after, bubble]
    if relay is not None:
        specs.append(whole)
        operands.append(relay)
    if base is not None:
        specs.append(block if has_base else pl.BlockSpec(memory_space=pl.ANY))
        operands.append(base)
    return pl.pallas_call(
        functools.partial(crossed_kernel, relay is not None, has_base),
        grid_spec=pltpu.PrefetchScalarGridSpec(
            num_scalar_prefetch=2,
            grid=(slots,),
            in_specs=specs,
            out_specs=block,
            scratch_shapes=[
                pltpu.VMEM((padded, depth, lanes), jnp.float32),
                pltpu.VMEM((padded, depth, lanes), jnp.float32),
            ],
        ),
        out_shape=jax.ShapeDtypeStruct(vertex.shape, jnp.float32),
        input_output_aliases={} if base is None else {len(operands) - 1: 0},
        compiler_params=pltpu.CompilerParams(vmem_limit_bytes=vmem_bytes),
        cost_estimate=cost(10),
        name="crossed",
    )(*operands)


def coupling_matrices(neighbours, pair_count):
    shards = lax.axis_size("pair")
    own = lax.axis_index("pair")
    pair_column = neighbours[:, 0]
    partner_column = neighbours[:, 1]
    sign_column = neighbours[:, 2]
    inner = lax.iota(jnp.int32, pair_count)
    left_ids = jnp.concatenate([(own ^ j) * pair_count + inner for j in range(shards)])
    right_ids = own * pair_count + inner
    partner_hits = (partner_column[:, None] == left_ids[None, :]).astype(jnp.bfloat16)
    pair_hits = jnp.where(
        pair_column[:, None] == right_ids[None, :], sign_column[:, None], 0
    ).astype(jnp.bfloat16)
    signs = lax.dot_general(
        partner_hits, pair_hits, (((0,), (0,)), ((), ())), preferred_element_type=jnp.float32
    )
    return signs.astype(jnp.bfloat16).reshape(shards, pair_count, pair_count)


def section_of(vertex, bubble, stencil, rows, places, more, neighbours):
    slots, components, width, depth, pairs = vertex.shape
    shards = lax.axis_size("pair")
    devices = lax.axis_size("freq")
    last = depth_z - 1
    onward = [(i, i + 1) for i in range(devices - 1)]
    backward = [(j, i) for i, j in onward]
    onward_inside = [(i, j) for i, j in onward if i % depth_z != last]
    backward_inside = [(j, i) for i, j in onward_inside]
    steps = [(i, j) for i, j in onward if i % depth_z == last]
    lend = [(i, i - 1) for i, _ in steps] + [(j, j + 1) for _, j in steps]
    wrap = [(i, i - last) for i, _ in steps] + [(j, j + last) for _, j in steps]
    sideways = [(i - last, j) for i, j in steps] + [(j + last, i) for i, j in steps]
    relay = [(i - 1, j) for i, j in steps] + [(j + 1, i) for i, j in steps]
    across = [(i, i ^ 2) for i in range(shards)]
    beside = [(i, i ^ 1) for i in range(shards)]
    chunks = [(1, 0), (1, 1), (0, 0), (0, 1)]

    every_row, rows = rows, rows[:main_rows]

    def add(section, j, sides, turned=None):
        component, half = chunks[j]
        return crossed(
            vertex, rows, places, stencil, *sides, scaled, component, half,
            component == 0, section, turned,
        )

    def add_more(turn, section):
        first = (turn + 1) * main_rows
        more_rows = lax.dynamic_slice(every_row, (first,), (width - main_rows,))
        for component, half in chunks:
            section = crossed(
                vertex, more_rows, places - first, stencil,
                *halo(pack(vertex, more_rows, component, half)), scaled, component, half,
                True, section,
            )
        return section

    def halo(packed):
        return lax.ppermute(packed, "freq", onward), lax.ppermute(packed, "freq", backward)

    spin = vertex[:, 0]
    scaled = jnp.broadcast_to((step_size * bubble)[:, :, None], (slots, depth, lanes))
    packed = [pack(vertex, rows, component, half) for component, half in chunks]
    density = pack(vertex, rows, 1)
    near = lax.ppermute(spin, "pair", beside)
    stage = (
        lax.ppermute(spin, "pair", across),
        near,
        lax.ppermute(packed[0], "freq", lend),
        lax.ppermute(density, "freq", onward_inside),
        lax.ppermute(density, "freq", backward_inside),
        lax.ppermute(lax.optimization_barrier((packed[1], near))[0], "freq", wrap),
        coupling_matrices(neighbours, pairs),
        *packed[2:],
    )
    far, near, lent, before, behind, wrapped, coupling, *packed = lax.optimization_barrier(stage)
    section = lattice(vertex, near, far, lax.ppermute(far, "pair", beside), coupling, scaled)
    section = add(section, 1, (before, behind), lax.ppermute(wrapped, "freq", sideways))
    sides_2 = halo(packed[0])
    stage = (lax.ppermute(lent, "freq", relay), section, packed[1])
    relayed, section, packed_3 = lax.optimization_barrier(stage)
    sides_3 = halo(packed_3)
    section = add(section, 0, (before, behind), relayed)
    section = add(section, 2, sides_2)
    section = add(section, 3, sides_3)
    return lax.fori_loop(0, more, add_more, section)


def body(vertex, bubble, stencil, freq_map, neighbours):
    width = vertex.shape[2]
    ids = lax.iota(jnp.int32, width)
    picked = freq_map[:, None] == ids[None, :]
    used = jnp.any(picked, axis=0)
    rank = jnp.sum(jnp.where(used[:, None] & (ids[:, None] <= ids[None, :]), 1, 0), axis=0) - 1
    rows = jnp.sum(jnp.where(used[:, None] & (rank[:, None] == ids[None, :]), ids[:, None], 0), axis=0)
    places = jnp.sum(jnp.where(picked, rank[None, :], 0), axis=1)
    count = rank[width - 1] + 1

    more = (count > main_rows).astype(jnp.int32)
    return section_of(vertex, bubble, stencil, rows, places, more, neighbours)


def solution(mesh):
    in_specs = (P("freq", None, None, None, "pair"), P("freq", None), P("freq", None), P(), P())
    out_specs = P("freq", None, None, None, "pair")
    return jax.shard_map(body, mesh=mesh, in_specs=in_specs, out_specs=out_specs, check_vma=False)
```
